128 devices in a mesh: row: 8 (over x, core), col: 16 (over z, y).
Axes of the slice: x: 4, y: 4, z: 4, core: 2. Of those that a mesh axis runs over, the one named last changes fastest.
Arguments:
- factor_trail: bfloat16 [256, 4, 1024, 1024], P(('row', 'col')), may hold values from -0.09375 to 0.09375
- pattern: int32 [256, 4], P(('row', 'col')), may hold values 0 or 1
- rhs_trail: bfloat16 [256, 1024, 512], P(('row', 'col')), may hold values from -6 to 6
- coupling: bfloat16 [4, 4, 1024, 1024], P(None, None, 'row', 'col'), may hold values from -0.125 to 0.125
- diag_inverse: float32 [4, 1024, 1024], P(None, 'col', 'row'), may hold values from -1.5 to 1.5, as said below
- rhs_super: float32 [4, 1024, 512], P(None, 'row'), may hold values from -6 to 6
Outputs:
- solved_blocks: bfloat16 [4, 1024, 512], P(None, 'col')
- updated_trail: float32 [256, 1024, 512], P(('row', 'col'))
The draws below stay inside these ranges and needn't reach their ends.
Inputs may be any that keep to these rules, and one draw needn't show every extreme that they name: Each diag_inverse[j] is lower triangular with diagonal entries between 0.75 and 1.35.
All inputs are finite; a program needn't handle non-finite values. No bound on the sum of `pattern` on one device may be relied on, other than what follows from the above.
Results may differ from the reference program's by a relative error of at most 0.0049.
Values may be sent and summed in bfloat16 or wider, within the bound.
No kernel may reach another device: no remote copies, remote signals or barrier semaphores. Data moves between devices by JAX's collectives and lax.ppermute only.
A program may use at most 128 MiB of HBM per device.

```python
import math
import jax
import jax.numpy as jnp
from jax import lax

B = 1024
K = 4
NRHS = 512
NBR = 256


def draw_diag_inverse(key, part):
    first_key, second_key = jax.random.split(key)
    rows_index = lax.broadcasted_iota(jnp.int32, (K, B, B), 1)
    cols_index = lax.broadcasted_iota(jnp.int32, (K, B, B), 2)
    noise = jnp.clip(jax.random.normal(first_key, (K, B, B), jnp.float32), -4.0, 4.0)
    diagonal = jax.random.uniform(second_key, (K, B, B), jnp.float32, 0.85, 1.25)
    scaled = noise * (0.5 / math.sqrt(B))
    lower = jnp.where(rows_index > cols_index, scaled, jnp.zeros_like(scaled))
    return jnp.where(rows_index == cols_index, diagonal, lower).astype(jnp.float32)


def place_ends(array, stream_key, low, top_value):
    dims = array.shape
    index_at = [jax.random.randint(jax.random.fold_in(stream_key, axis), (), 0, dims[axis]) for axis in range(len(dims))]
    array = array.at[tuple(index_at)].set(low)
    longest = dims.index(max(dims))
    index_at[longest] = (index_at[longest] + 1) % dims[longest]
    return array.at[tuple(index_at)].set(top_value)


def level_of(own_key, shape, shards, low, largest):
    def one(dim, parts):
        heights = jax.random.uniform(jax.random.fold_in(jax.random.fold_in(own_key, 6), dim), (parts,), jnp.float32, low / len(shards), largest / len(shards))
        return jnp.repeat(jnp.exp(heights), shape[dim] // parts).reshape((-1,) + (1,) * (len(shape) - dim - 1))

    level = one(*shards[0])
    for cut in shards[1:]:
        level = level * one(*cut)
    return level


def centred(own_key, shape, scale, most, cuts=(), kind=jnp.bfloat16):
    array = jax.random.normal(own_key, shape, jnp.float32) * scale
    if len(cuts) > 0:
        array = level_of(own_key, shape, cuts, -0.22, 0.18) * array
    return jnp.clip(array, min=-most, max=most).astype(kind)


def setup_inputs(seed: int = 0) -> dict:
    keys = jax.random.split(jax.random.key(seed), 7)
    factor_trail = centred(keys[0], (NBR, K, B, B), (K * B) ** -0.5, 0.09375, ((0, 128),))
    pattern = place_ends((jax.random.randint(keys[1], (NBR, K), 0, 2) < 1).astype(jnp.int32), jax.random.fold_in(keys[1], 1), 0, 1)
    rhs_trail = centred(keys[2], (NBR, B, NRHS), 1.0, 6.0, ((0, 128),))
    coupling = centred(keys[3], (K, K, B, B), (2 * B) ** -0.5, 0.125, ((2, 8), (3, 16)))
    diag_inverse = draw_diag_inverse(jax.random.fold_in(keys[6], 71), 0)
    rhs_super = centred(keys[5], (K, B, NRHS), 1.0, 6.0, ((1, 8),), jnp.float32)
    return dict(factor_trail=factor_trail, pattern=pattern, rhs_trail=rhs_trail, coupling=coupling, diag_inverse=diag_inverse, rhs_super=rhs_super)


def reference(factor_trail, pattern, rhs_trail, coupling, diag_inverse, rhs_super):
    solved = []
    for column in range(K):
        right_block = rhs_super[column]
        for earlier in range(column):
            right_block = right_block - jnp.dot(coupling[column, earlier], solved[earlier], preferred_element_type=jnp.float32)
        value = jnp.dot(diag_inverse[column], right_block, precision=lax.Precision.HIGHEST, preferred_element_type=jnp.float32)
        solved.append(value.astype(jnp.bfloat16))
    stacked = jnp.stack(solved).astype(jnp.float32)

    def one_row(inputs):
        blocks, mask_row = inputs
        masked = mask_row.astype(jnp.float32)[:, None, None] * stacked
        return jnp.einsum("jab,jbn->an", blocks.astype(jnp.float32), masked, precision=lax.Precision.HIGHEST)

    updates_sum = lax.map(one_row, (factor_trail, pattern))
    updated_trail = rhs_trail.astype(jnp.float32) - updates_sum
    return jnp.stack(solved), updated_trail
```

```python
import jax
import jax.numpy as jnp
from jax import lax
from jax.experimental import pallas as pl
from jax.experimental.pallas import tpu as pltpu
from jax.sharding import Mesh
from jax.sharding import PartitionSpec as P

NT = (((1,), (1,)), ((), ()))
NN = (((1,), (0,)), ((), ()))
VMEM_LIMIT = 48 * 1024 * 1024


def dot(a, b, dims):
    return lax.dot_general(a, b, dims, preferred_element_type=jnp.float32)


def split(value):
    high = value.astype(jnp.bfloat16)
    low = (value - high.astype(jnp.float32)).astype(jnp.bfloat16)
    return high, low


def apply_inverse(right, high_ref_value, low_ref_value):
    high, low = split(right)
    return (
        dot(high, high_ref_value, NT)
        + dot(low, high_ref_value, NT)
        + dot(high, low_ref_value, NT)
    )


def first_kernel(right_ref, inverse_ref, out_ref):
    rows = inverse_ref.shape[0] * inverse_ref.shape[2]
    depth = inverse_ref.shape[3]
    high = inverse_ref[:, 0].reshape(rows, depth)
    low = inverse_ref[:, 1].reshape(rows, depth)
    out_ref[...] = apply_inverse(right_ref[...], high, low)


def step_kernel(column, at, n_parts, *refs):
    part_refs = refs[:n_parts]
    right_ref = refs[n_parts]
    mine_ref, other_ref = refs[n_parts + 1 : n_parts + 3]
    earlier_refs = refs[n_parts + 3 : n_parts + 3 + column - 1]
    solved_ref, out_ref = refs[-2:]
    total = part_refs[0][...]
    for part in part_refs[1:]:
        total = total + part[...]
    solved = total.astype(jnp.bfloat16)
    solved_ref[...] = solved
    before = [ref[...] for ref in earlier_refs] + [solved]
    out = None
    for side, ref in enumerate((mine_ref, other_ref)):
        rows = ref.shape[0] * ref.shape[2]
        depth = ref.shape[3]
        right = right_ref[side]
        for i, block in enumerate(before):
            right = right - dot(block, ref[:, at + 2 + i].reshape(rows, depth), NN)
        term = apply_inverse(
            right, ref[:, at].reshape(rows, depth), ref[:, at + 1].reshape(rows, depth)
        )
        out = term if out is None else out + term
    out_ref[...] = out


def last_kernel(*refs):
    total = refs[0][...]
    for part in refs[1:-1]:
        total = total + part[...]
    refs[-1][...] = total.astype(jnp.bfloat16)


def trail_kernel(first, pattern_ref, base_ref, factor_ref, *refs):
    solved_refs, out_ref = refs[:-1], refs[-1]
    row = pl.program_id(0)
    total = base_ref[0].astype(jnp.float32)
    for k, ref in enumerate(solved_refs):
        weight = pattern_ref[row, first + k].astype(jnp.float32)
        total = total - weight * dot(factor_ref[0, k], ref[...], NT)
    out_ref[0] = total


def trail(first, pattern, base, factor, solved, tile):
    count = len(solved)
    n_rows, height, width = base.shape
    depth = factor.shape[3]
    full = pl.BlockSpec((width, depth), lambda r, a: (0, 0))
    block = first // count
    return pl.pallas_call(
        lambda *refs: trail_kernel(first, *refs),
        grid=(n_rows, height // tile),
        in_specs=[
            pl.BlockSpec(memory_space=pltpu.SMEM),
            pl.BlockSpec((1, tile, width), lambda r, a: (r, a, 0)),
            pl.BlockSpec((1, count, tile, depth), lambda r, a: (r, block, a, 0)),
        ]
        + [full] * count,
        out_specs=pl.BlockSpec((1, tile, width), lambda r, a: (r, a, 0)),
        out_shape=jax.ShapeDtypeStruct(base.shape, jnp.float32),
        compiler_params=pltpu.CompilerParams(vmem_limit_bytes=VMEM_LIMIT),
        cost_estimate=pl.CostEstimate(
            flops=2 * n_rows * height * width * depth * count,
            bytes_accessed=2 * n_rows * height * depth * count,
            transcendentals=0,
        ),
        name="trail",
    )(pattern, base, factor, *solved)


def small_call(kernel, outs, *operands, name):
    return pl.pallas_call(
        kernel,
        out_shape=outs,
        in_specs=[pl.BlockSpec(memory_space=pltpu.VMEM)] * len(operands),
        out_specs=jax.tree.map(lambda _: pl.BlockSpec(memory_space=pltpu.VMEM), outs),
        compiler_params=pltpu.CompilerParams(vmem_limit_bytes=VMEM_LIMIT),
        cost_estimate=pl.CostEstimate(
            flops=2**28, bytes_accessed=2**21, transcendentals=0
        ),
        name=name,
    )(*operands)


def make(sizes):
    n_x, n_core, n_z, n_y = sizes
    n_col = n_z * n_y
    n_part = n_core * n_col

    def swap(value):
        return lax.ppermute(value, "core", [(i, n_core - 1 - i) for i in range(n_core)])

    def spread(value, axes, count):
        return lax.all_to_all(
            jnp.broadcast_to(value[None], (count, *value.shape)), axes, 0, 0
        )

    def parts_over_x(value):
        return [value] + [
            lax.ppermute(value, "x", [(i, (i + k) % n_x) for i in range(n_x)])
            for k in (1, n_x - 1, 2)
        ]

    def per_device(factor, pattern, rhs_trail, coupling, inverse, rhs):
        columns, height, width = rhs.shape
        share = width // n_part
        core = lax.axis_index("core")
        col = lax.axis_index("z") * n_y + lax.axis_index("y")

        def columns_of(which):
            at = (which * n_col + col) * share
            return lax.dynamic_slice(
                rhs, (0, 0, at), (columns, height, share)
            ).transpose(0, 2, 1)

        high = lax.reduce_precision(inverse, 8, 7)
        low = (inverse - high).astype(jnp.bfloat16)
        high = high.astype(jnp.bfloat16)
        across = coupling.transpose(0, 1, 3, 2)

        def pack(column):
            return [high[column], low[column]] + [across[column, i] for i in range(column)]

        mine_right = columns_of(core)
        other_right = columns_of(1 - core)
        inverse0 = spread(jnp.stack(pack(0)), ("z", "y"), n_col)
        group1 = spread(jnp.stack(pack(1)), ("z", "y"), n_col)
        group2 = spread(jnp.stack(pack(2) + pack(3)), ("z", "y"), n_col)
        rights = jnp.stack([mine_right, swap(other_right)], axis=1)
        block = n_col * inverse.shape[1]
        partial_shape = jax.ShapeDtypeStruct((share, block), jnp.float32)
        solved_shape = jax.ShapeDtypeStruct((share, block), jnp.bfloat16)

        both = small_call(
            first_kernel,
            jax.ShapeDtypeStruct((2 * share, block), jnp.float32),
            jnp.concatenate([mine_right[0], other_right[0]], axis=0),
            inverse0,
            name="first",
        )
        partial_sum = both[:share] + swap(both[share:])
        groups = {1: (group1, swap(group1), 0), 2: (group2, swap(group2), 0)}
        groups[3] = (*groups[2][:2], 4)
        pieces, whole = [], []
        for column in range(1, columns):
            mine, other, at = groups[column]
            parts = parts_over_x(partial_sum)
            solved, partial_sum = small_call(
                lambda *refs, c=column, a=at, n=len(parts): step_kernel(c, a, n, *refs),
                (solved_shape, partial_shape),
                *parts,
                rights[column],
                mine,
                other,
                *pieces,
                name="step",
            )
            pieces.append(solved)
            whole.append(spread(solved, ("core", "z", "y"), n_part).reshape(width, block))
        last = small_call(
            last_kernel, solved_shape, *parts_over_x(partial_sum), name="last"
        )
        base = trail(0, pattern, rhs_trail, factor, whole, 256)
        whole.append(spread(last, ("core", "z", "y"), n_part).reshape(width, block))
        updated = trail(3, pattern, base, factor, whole[3:], 512)
        own = block // n_col
        solved_blocks = jnp.stack(
            [lax.dynamic_slice(w, (0, col * own), (width, own)).T for w in whole]
        )
        return solved_blocks, updated

    return per_device


def solution(mesh):
    row, col = mesh.shape["row"], mesh.shape["col"]
    n_x, n_z = row // 2, 4
    n_y = col // n_z
    sizes = (n_x, 2, n_z, n_y)
    fine = Mesh(mesh.devices.reshape(sizes), ("x", "core", "z", "y"))
    r, c = ("x", "core"), ("z", "y")
    return jax.shard_map(
        make(sizes),
        mesh=fine,
        in_specs=(
            P(r + c, None, None, None),
            P(r + c, None),
            P(r + c, None, None),
            P(None, None, r, c),
            P(None, c, r),
            P(None, r, None),
        ),
        out_specs=(P(None, c, None), P(r + c, None, None)),
        check_vma=False,
    )
```

```python
import jax
import jax.numpy as jnp
from jax import lax
from jax.experimental import pallas as pl
from jax.experimental.pallas import tpu as pltpu
from jax.sharding import Mesh
from jax.sharding import PartitionSpec as P

NT = (((1,), (1,)), ((), ()))
NN = (((1,), (0,)), ((), ()))
MIB = 1024 * 1024
EARLY = ((0, None), (1, None), (1, 0))
LATE = ((2, None), (2, 0), (2, 1), (3, None), (3, 0), (3, 1), (3, 2))


def dot(a, b, dims):
    return lax.dot_general(a, b, dims, preferred_element_type=jnp.float32)


def call(kernel, outs, *operands, name, scalars=0, scratch=(), after=(), limit=24):
    vmem = pl.BlockSpec(memory_space=pltpu.VMEM)
    smem = pl.BlockSpec(memory_space=pltpu.SMEM)
    unread = pl.BlockSpec(memory_space=pl.ANY)
    count = len(operands)
    return pl.pallas_call(
        lambda *refs: kernel(*refs[:count], *refs[count + len(after) :]),
        out_shape=outs,
        in_specs=[smem] * scalars + [vmem] * (count - scalars) + [unread] * len(after),
        out_specs=jax.tree.map(lambda _: vmem, outs),
        scratch_shapes=list(scratch),
        compiler_params=pltpu.CompilerParams(vmem_limit_bytes=limit * MIB),
        cost_estimate=pl.CostEstimate(
            flops=2**28, bytes_accessed=2**21, transcendentals=0
        ),
        name=name,
    )(*operands, *after)


def pack_kernel(members, place_ref, inverse_ref, coupling_ref, out_ref):
    copies = out_ref.shape[0]
    columns, rows, width = inverse_ref.shape
    depth = coupling_ref.shape[3]
    eye = (
        lax.broadcasted_iota(jnp.int32, (depth, depth), 0)
        == lax.broadcasted_iota(jnp.int32, (depth, depth), 1)
    ).astype(jnp.bfloat16)
    blocks = []
    lowest = min(column for column, earlier in members if earlier is not None)
    for column, earlier in members:
        if earlier is None:
            blocks.append(inverse_ref[column].astype(jnp.bfloat16))
        else:
            blocks.append(
                dot(eye, coupling_ref[column - lowest, earlier], NT).astype(jnp.bfloat16)
            )
    if members[0][0] == 0:
        first_row, first_lane = place_ref[0] * rows, place_ref[1] * width
        on_diagonal = (
            lax.broadcasted_iota(jnp.int32, (rows, width), 0) + first_row
            == lax.broadcasted_iota(jnp.int32, (rows, width), 1) + first_lane
        )
        at_row = lax.broadcasted_iota(jnp.int32, (16, width), 0)
        tile = jnp.zeros((16, width), jnp.float32)
        for column in range(columns):
            value = inverse_ref[column]
            rest = value - value.astype(jnp.bfloat16).astype(jnp.float32)
            line = jnp.sum(jnp.where(on_diagonal, rest, 0.0), axis=0, keepdims=True)
            tile = tile + jnp.where(at_row == column, line, 0.0)
        blocks.append(tile.astype(jnp.bfloat16))
    whole = jnp.concatenate(blocks, axis=0)
    for copy in range(copies):
        out_ref[copy] = whole


def pack(members, copies, place, inverse, coupling, after=()):
    count = len(members) * inverse.shape[1] + (16 if members[0][0] == 0 else 0)
    return call(
        lambda *refs: pack_kernel(members, *refs),
        jax.ShapeDtypeStruct((copies, count, inverse.shape[2]), jnp.bfloat16),
        place,
        inverse,
        coupling,
        scalars=1,
        after=after,
        name="pack",
    )


def block_of(ref, at, size):
    return ref[:, at : at + size].reshape(ref.shape[0] * size, ref.shape[2])


def rest_of(early_ref, column):
    tiles = early_ref[:, early_ref.shape[1] - 16 :].astype(jnp.float32)
    return jnp.sum(tiles, axis=0)[column : column + 1]


def apply_inverse(right, inverse, rest, slab, out_ref, add):
    count, width = right.shape
    high = right.astype(jnp.bfloat16)
    low = (right - high.astype(jnp.float32)).astype(jnp.bfloat16)
    both = dot(jnp.concatenate([high, low], axis=0), inverse, NT)
    value = both[:count] + both[count:]
    out_ref[...] = out_ref[...] + value if add else value
    lanes = pl.ds(pl.multiple_of(slab * width, width), width)
    out_ref[:, lanes] = out_ref[:, lanes] + right * rest


def first_kernel(size, place_ref, right_ref, early_ref, keep_ref, give_ref, mark_ref, out_ref):
    apply_inverse(
        right_ref[...],
        block_of(early_ref, 0, size),
        rest_of(early_ref, 0),
        place_ref[1],
        out_ref,
        False,
    )
    core = place_ref[2]
    count = keep_ref.shape[0]
    keep_ref[...] = out_ref[pl.ds(pl.multiple_of(core * count, count), count)]
    give_ref[...] = out_ref[pl.ds(pl.multiple_of((1 - core) * count, count), count)]
    mark_ref[...] = right_ref[: mark_ref.shape[0]]


def halves(solved_ref, core, keep_ref, give_ref):
    half = keep_ref.shape[1]
    keep_ref[...] = solved_ref[:, pl.ds(pl.multiple_of(core * half, half), half)]
    give_ref[...] = solved_ref[:, pl.ds(pl.multiple_of((1 - core) * half, half), half)]


def close_kernel(place_ref, *refs):
    part_refs, (solved_ref, keep_ref, give_ref, mark_ref) = refs[:-4], refs[-4:]
    total = part_refs[0][...]
    for part in part_refs[1:]:
        total = total + part[...]
    solved_ref[...] = total.astype(jnp.bfloat16)
    halves(solved_ref, place_ref[2], keep_ref, give_ref)
    mark_ref[...] = total[: mark_ref.shape[0], : mark_ref.shape[1]]


def step_kernel(column, at, size, place_ref, right_ref, *refs):
    early_refs, group_refs, solved_refs, out_ref = refs[:2], refs[2:4], refs[4:-1], refs[-1]
    slabs = (place_ref[1], place_ref[1] + 1 - 2 * place_ref[2])
    skip = 2 * size if column == 1 else size
    for side in range(2):
        right = right_ref[column, side]
        for i, block_ref in enumerate(solved_refs):
            right = right - dot(
                block_ref[...], block_of(group_refs[side], at + skip + i * size, size), NN
            )
        apply_inverse(
            right,
            block_of(group_refs[side], at + skip - size, size),
            rest_of(early_refs[side], column),
            slabs[side],
            out_ref,
            side > 0,
        )


def bundle_kernel(place_ref, *refs):
    core = place_ref[2]
    out_ref = refs[-1]
    for k in range(len(refs) // 2):
        keep, got = refs[2 * k][...], refs[2 * k + 1][...]
        for copy in range(out_ref.shape[0]):
            out_ref[copy, k, core] = keep
            out_ref[copy, k, 1 - core] = got


def trail_kernel(columns, pattern_ref, place_ref, base_ref, mine_ref, other_ref, *refs):
    count = len(columns)
    factor_refs, (out_ref, own_ref) = refs[:count], refs[count:]
    row = pl.program_id(0)
    core = place_ref[2]
    width, half = out_ref.shape[2], mine_ref.shape[4]
    offsets = [
        pl.multiple_of(core * half, half),
        pl.multiple_of((1 - core) * half, half),
    ]

    def solved(ref, k):
        return ref[:, k].reshape(width, half)

    total = base_ref[0].astype(jnp.float32)
    for k, column in enumerate(columns):
        product = None
        for ref, offset in zip((mine_ref, other_ref), offsets):
            factor = factor_refs[k][0, 0, :, pl.ds(offset, half)]
            term = dot(factor, solved(ref, k), NT)
            product = term if product is None else product + term
        total = total - pattern_ref[row, column].astype(jnp.float32) * product
    out_ref[0] = total

    @pl.when((row == 0) & (pl.program_id(1) == 0))
    def _():
        own = own_ref.shape[1]
        lane = lax.broadcasted_iota(jnp.int32, (own, half), 1)
        wanted = lax.broadcasted_iota(jnp.int32, (own, half), 0) + place_ref[0] * own
        for k in range(count):
            rows = None
            for ref, offset in zip((mine_ref, other_ref), offsets):
                pick = (lane + offset == wanted).astype(jnp.bfloat16)
                term = dot(pick, solved(ref, k), NT)
                rows = term if rows is None else rows + term
            own_ref[k] = rows.astype(jnp.bfloat16)


def trail(columns, pattern, place, base, factor, mine, other, own, tile):
    n_rows, height, width = base.shape
    depth = factor.shape[3]
    count = len(columns)

    def factor_spec(column):
        return pl.BlockSpec((1, 1, tile, depth), lambda r, a: (r, column, a, 0))

    smem = pl.BlockSpec(memory_space=pltpu.SMEM)
    vmem = pl.BlockSpec(memory_space=pltpu.VMEM)
    row_tile = pl.BlockSpec((1, tile, width), lambda r, a: (r, a, 0))
    return pl.pallas_call(
        lambda *refs: trail_kernel(columns, *refs),
        grid=(n_rows, height // tile),
        in_specs=[smem, smem, row_tile, vmem, vmem]
        + [factor_spec(column) for column in columns],
        out_specs=[
            row_tile,
            pl.BlockSpec((count, own, width), lambda r, a: (0, 0, 0)),
        ],
        out_shape=[
            jax.ShapeDtypeStruct(base.shape, jnp.float32),
            jax.ShapeDtypeStruct((count, own, width), jnp.bfloat16),
        ],
        compiler_params=pltpu.CompilerParams(vmem_limit_bytes=40 * MIB),
        cost_estimate=pl.CostEstimate(
            flops=2 * n_rows * height * width * depth * count,
            bytes_accessed=2 * n_rows * height * depth * count,
            transcendentals=0,
        ),
        name="trail",
    )(pattern, place, base, mine, other, *([factor] * count))


def make(sizes):
    n_x, n_core, n_z, n_y = sizes
    n_col = n_z * n_y

    def swap(value):
        return lax.ppermute(value, "core", [(i, n_core - 1 - i) for i in range(n_core)])

    def exchange(value):
        return lax.all_to_all(value, ("z", "y"), 0, 0)

    def parts_over_x(value):
        return [value] + [
            lax.ppermute(value, "x", [(i, (i + k) % n_x) for i in range(n_x)])
            for k in (1, n_x - 1, 2)
        ]

    def per_device(factor, pattern, rhs_trail, coupling, inverse, rhs):
        columns, height, width = rhs.shape
        share = width // (n_core * n_col)
        size = inverse.shape[1]
        block = n_col * size
        core = lax.axis_index("core")
        col = lax.axis_index("z") * n_y + lax.axis_index("y")
        place = jnp.stack([col, lax.axis_index("x") * n_core + core, core])

        tied = lax.optimization_barrier
        packed = pack(EARLY, n_col, place, inverse, coupling[1:2, 0:1])
        early = exchange(packed)
        packed_late = pack(LATE, n_col, place, inverse, coupling[2:], after=[packed])
        right = lax.dynamic_slice(
            rhs, (0, 0, col * n_core * share), (columns, height, n_core * share)
        ).transpose(0, 2, 1)
        rights = [
            lax.dynamic_slice(right, (0, which * share, 0), (columns, share, height))
            for which in (core, 1 - core)
        ]
        rights = jnp.stack([rights[0], swap(rights[1])], axis=1)

        partial_shape = jax.ShapeDtypeStruct((share, block), jnp.float32)
        solved_shape = jax.ShapeDtypeStruct((share, block), jnp.bfloat16)
        half_shape = jax.ShapeDtypeStruct((share, block // n_core), jnp.bfloat16)
        mark_shape = jax.ShapeDtypeStruct((8, 128), jnp.float32)
        early_both = (early, swap(early))
        keep, give, mark = call(
            lambda *refs: first_kernel(size, *refs),
            (partial_shape, partial_shape, mark_shape),
            place,
            right[0],
            early,
            scalars=1,
            scratch=[pltpu.VMEM((n_core * share, block), jnp.float32)],
            after=[rights, packed_late],
            name="first",
        )
        packed_late, mark = tied((packed_late, mark))
        late = exchange(packed_late)
        late_both = None
        partial_sum = keep + swap(give)
        pieces, sent = [], []
        for column in range(1, columns + 1):
            solved, keep, give, mark = call(
                close_kernel,
                (solved_shape, half_shape, half_shape, mark_shape),
                place,
                *parts_over_x(partial_sum),
                scalars=1,
                after=[mark],
                name="close",
            )
            pieces.append(solved)
            sent += [keep, swap(give)]
            if column == columns:
                break
            if column == 2:
                late, mark = tied((late, mark))
                late_both = (late, swap(late))
            group, at = (
                (early_both, 0),
                (late_both, 0),
                (late_both, 3 * size),
            )[column - 1]
            partial_sum = call(
                lambda *refs, c=column, a=at: step_kernel(c, a, size, *refs),
                partial_shape,
                place,
                rights,
                *early_both,
                *group,
                *pieces,
                scalars=1,
                after=[mark],
                name="step",
            )

        def send(halves_of, after):
            shape = (n_col, len(halves_of) // 2, n_core, share, block // n_core)
            return exchange(
                call(
                    bundle_kernel,
                    jax.ShapeDtypeStruct(shape, jnp.bfloat16),
                    place,
                    *halves_of,
                    scalars=1,
                    after=after,
                    name="bundle",
                )
            )

        first_pair, mark = tied((send(sent[:4], []), mark))
        second_pair = send(sent[4:], [mark])
        base, blocks01 = trail(
            (0, 1), pattern, place, rhs_trail, factor, first_pair, swap(first_pair), size, 512
        )
        second_pair, blocks01 = tied((second_pair, blocks01))
        updated, blocks23 = trail(
            (2, 3), pattern, place, base, factor, second_pair, swap(second_pair), size, 512
        )
        return jnp.concatenate([blocks01, blocks23]), updated

    return per_device


def solution(mesh):
    row, col = mesh.shape["row"], mesh.shape["col"]
    sizes = (row // 2, 2, 4, col // 4)
    fine = Mesh(mesh.devices.reshape(sizes), ("x", "core", "z", "y"))
    r, c = ("x", "core"), ("z", "y")
    return jax.shard_map(
        make(sizes),
        mesh=fine,
        in_specs=(
            P(r + c, None, None, None),
            P(r + c, None),
            P(r + c, None, None),
            P(None, None, r, c),
            P(None, c, r),
            P(None, r, None),
        ),
        out_specs=(P(None, c, None), P(r + c, None, None)),
        check_vma=False,
    )
```

```python
import jax
import jax.numpy as jnp
from jax import lax
from jax.experimental import pallas as pl
from jax.experimental.pallas import tpu as pltpu
from jax.sharding import Mesh
from jax.sharding import PartitionSpec as P

NT = (((1,), (1,)), ((), ()))
NN = (((1,), (0,)), ((), ()))
MIB = 1024 * 1024
EARLY = ((0, None), (1, None), (1, 0))
LATE = ((2, None), (2, 0), (2, 1), (3, None), (3, 0), (3, 1), (3, 2))
REST = 16


def core_of():
    return lax.axis_index("core")


def slab_of(core):
    return lax.axis_index("x") * lax.axis_size("core") + core


def col_of():
    return lax.axis_index("z") * lax.axis_size("y") + lax.axis_index("y")


def dot(a, b, dims):
    return lax.dot_general(a, b, dims, preferred_element_type=jnp.float32)


def call(kernel, outs, *operands, name, scratch=(), after=(), limit=24):
    vmem = pl.BlockSpec(memory_space=pltpu.VMEM)
    unread = pl.BlockSpec(memory_space=pl.ANY)
    count = len(operands)
    return pl.pallas_call(
        lambda *refs: kernel(*refs[:count], *refs[count + len(after) :]),
        out_shape=outs,
        in_specs=[vmem] * count + [unread] * len(after),
        out_specs=jax.tree.map(lambda _: vmem, outs),
        scratch_shapes=list(scratch),
        compiler_params=pltpu.CompilerParams(vmem_limit_bytes=limit * MIB),
        cost_estimate=pl.CostEstimate(
            flops=2**28, bytes_accessed=2**21, transcendentals=0
        ),
        name=name,
    )(*operands, *after)


def pack_kernel(members, inverse_ref, across_ref, out_ref):
    columns, rows, width = inverse_ref.shape
    blocks = []
    for column, earlier in members:
        if earlier is None:
            blocks.append(inverse_ref[column].astype(jnp.bfloat16))
        else:
            blocks.append(across_ref[column, earlier])
    if members[0][0] == 0:
        first_row, first_lane = col_of() * rows, slab_of(core_of()) * width
        on_diagonal = (
            lax.broadcasted_iota(jnp.int32, (rows, width), 0) + first_row
            == lax.broadcasted_iota(jnp.int32, (rows, width), 1) + first_lane
        )
        at_row = lax.broadcasted_iota(jnp.int32, (REST, width), 0)
        tile = jnp.zeros((REST, width), jnp.float32)
        for column in range(columns):
            value = inverse_ref[column]
            rest = value - value.astype(jnp.bfloat16).astype(jnp.float32)
            line = jnp.sum(jnp.where(on_diagonal, rest, 0.0), axis=0, keepdims=True)
            tile = tile + jnp.where(at_row == column, line, 0.0)
        blocks.append(tile.astype(jnp.bfloat16))
    whole = jnp.concatenate(blocks, axis=0)
    for copy in range(out_ref.shape[0]):
        out_ref[copy] = whole


def pack(members, copies, inverse, across, after=()):
    count = len(members) * inverse.shape[1] + (REST if members[0][0] == 0 else 0)
    return call(
        lambda *refs: pack_kernel(members, *refs),
        jax.ShapeDtypeStruct((copies, count, inverse.shape[2]), jnp.bfloat16),
        inverse,
        across,
        after=after,
        name="pack",
    )


def block_of(ref, at, size):
    return ref[:, at : at + size].reshape(ref.shape[0] * size, ref.shape[2])


def rest_of(ref, column):
    tiles = ref[:, ref.shape[1] - REST :].astype(jnp.float32)
    return jnp.sum(tiles, axis=0)[column : column + 1]


def apply_inverse(right, inverse, rest, slab, out_ref, add):
    count, width = right.shape
    high = right.astype(jnp.bfloat16)
    low = (right - high.astype(jnp.float32)).astype(jnp.bfloat16)
    both = dot(jnp.concatenate([high, low], axis=0), inverse, NT)
    value = both[:count] + both[count:]
    out_ref[...] = out_ref[...] + value if add else value
    lanes = pl.ds(pl.multiple_of(slab * width, width), width)
    out_ref[:, lanes] = out_ref[:, lanes] + right * rest


def first_kernel(
    size, right_ref, group_ref, keep_ref, give_ref, mark_ref, out_ref
):
    apply_inverse(
        right_ref[...],
        block_of(group_ref, 0, size),
        rest_of(group_ref, 0),
        slab_of(core_of()),
        out_ref,
        False,
    )
    core = core_of()
    count = keep_ref.shape[0]
    keep_ref[...] = out_ref[pl.ds(pl.multiple_of(core * count, count), count)]
    give_ref[...] = out_ref[pl.ds(pl.multiple_of((1 - core) * count, count), count)]
    mark_ref[...] = right_ref[: mark_ref.shape[0]]


def part_kernel(start, group_ref, out_ref):
    out_ref[...] = group_ref[:, start : start + out_ref.shape[1]]


def part(group, start, length, after):
    shape = (group.shape[0], length, group.shape[2])
    return call(
        lambda *refs: part_kernel(start, *refs),
        jax.ShapeDtypeStruct(shape, group.dtype),
        group,
        after=after,
        name="part",
    )


def halves(solved_ref, core, keep_ref, give_ref):
    half = keep_ref.shape[1]
    keep_ref[...] = solved_ref[:, pl.ds(pl.multiple_of(core * half, half), half)]
    give_ref[...] = solved_ref[:, pl.ds(pl.multiple_of((1 - core) * half, half), half)]


def close_kernel(n_parts, *refs):
    part_refs, before_refs = refs[:n_parts], refs[n_parts:-4]
    solved_ref, keep_ref, give_ref, mark_ref = refs[-4:]
    total = part_refs[0][...]
    for part_ref in part_refs[1:]:
        total = total + part_ref[...]
    last = solved_ref.shape[0] - 1
    for ref in before_refs:
        solved_ref[:last] = ref[...]
    solved_ref[last] = total.astype(jnp.bfloat16)
    halves(solved_ref.at[last], core_of(), keep_ref, give_ref)
    mark_ref[...] = total[: mark_ref.shape[0], : mark_ref.shape[1]]


def step_kernel(column, starts, size, state_ref, solved_ref, *refs):
    group_refs, out_ref = refs[:2], refs[2]
    columns = state_ref.shape[0]
    if column == 1:
        next_ref = refs[3]
        next_ref[:columns] = state_ref[...]
        for side, ref in enumerate(group_refs):
            tiles = ref[:, ref.shape[1] - REST :].astype(jnp.float32)
            next_ref[columns, side] = jnp.sum(tiles, axis=0)
        state_ref, columns = next_ref, columns + 1
    slabs = (slab_of(core_of()), slab_of(1 - core_of()))
    for side, (ref, start) in enumerate(zip(group_refs, starts)):
        right = state_ref[column, side]
        for i in range(column):
            right = right - dot(
                solved_ref[i], block_of(ref, start + (1 + i) * size, size), NN
            )
        apply_inverse(
            right,
            block_of(ref, start, size),
            state_ref[columns - 1, side, column : column + 1],
            slabs[side],
            out_ref,
            side > 0,
        )


def bundle_kernel(*refs):
    core = core_of()
    out_ref, mark_ref = refs[-2:]
    for k in range(len(refs) // 2 - 1):
        keep, got = refs[2 * k][...], refs[2 * k + 1][...]
        for copy in range(out_ref.shape[0]):
            out_ref[copy, k, core] = keep
            out_ref[copy, k, 1 - core] = got
    mark_ref[...] = jnp.zeros(mark_ref.shape, mark_ref.dtype)


def trail_kernel(columns, before, pattern_ref, base_ref, mine_ref, other_ref, *refs):
    count = len(columns)
    factor_refs, (out_ref, own_ref) = refs[:count], refs[-2:]
    row = pl.program_id(0)
    core = core_of()
    width, half = out_ref.shape[2], mine_ref.shape[4]
    offsets = [
        pl.multiple_of(core * half, half),
        pl.multiple_of((1 - core) * half, half),
    ]

    def solved(ref, k):
        return ref[:, k].reshape(width, half)

    total = base_ref[0].astype(jnp.float32)
    for k, column in enumerate(columns):
        product = None
        for ref, offset in zip((mine_ref, other_ref), offsets):
            factor = factor_refs[k][0, 0, :, pl.ds(offset, half)]
            term = dot(factor, solved(ref, k), NT)
            product = term if product is None else product + term
        total = total - pattern_ref[row, column].astype(jnp.float32) * product
    out_ref[0] = total

    @pl.when((row == 0) & (pl.program_id(1) == 0))
    def _():
        own = own_ref.shape[1]
        lane = lax.broadcasted_iota(jnp.int32, (own, half), 1)
        wanted = lax.broadcasted_iota(jnp.int32, (own, half), 0) + col_of() * own
        if before:
            own_ref[:before] = refs[count][...]
        for k in range(count):
            rows = None
            for ref, offset in zip((mine_ref, other_ref), offsets):
                pick = (lane + offset == wanted).astype(jnp.bfloat16)
                term = dot(pick, solved(ref, k), NT)
                rows = term if rows is None else rows + term
            own_ref[before + k] = rows.astype(jnp.bfloat16)


def trail(columns, pattern, base, factor, mine, other, own, tile, done=(), after=()):
    n_rows, height, width = base.shape
    depth = factor.shape[-1]
    count, before = len(columns), sum(d.shape[0] for d in done)
    smem = pl.BlockSpec(memory_space=pltpu.SMEM)
    row_tile = pl.BlockSpec((1, tile, width), lambda r, a: (r, a, 0))

    def factor_spec(column):
        return pl.BlockSpec((1, 1, tile, depth), lambda r, a: (r, column, a, 0))

    def whole(shape):
        return pl.BlockSpec(shape, lambda r, a: (0,) * len(shape))

    held = 4 + count + len(done)
    own_shape = (before + count, own, width)
    return pl.pallas_call(
        lambda *refs: trail_kernel(columns, before, *refs[:held], *refs[-2:]),
        grid=(n_rows, height // tile),
        in_specs=[smem, row_tile, whole(mine.shape), whole(other.shape)]
        + [factor_spec(column) for column in columns]
        + [whole(d.shape) for d in done]
        + [pl.BlockSpec(memory_space=pl.ANY)] * len(after),
        out_specs=[row_tile, whole(own_shape)],
        out_shape=[
            jax.ShapeDtypeStruct(base.shape, jnp.float32),
            jax.ShapeDtypeStruct(own_shape, jnp.bfloat16),
        ],
        compiler_params=pltpu.CompilerParams(vmem_limit_bytes=58 * MIB),
        cost_estimate=pl.CostEstimate(
            flops=2 * n_rows * height * width * depth * count,
            bytes_accessed=2 * n_rows * height * depth * count,
            transcendentals=0,
        ),
        name="trail",
    )(pattern, base, mine, other, *([factor] * count), *done, *after)


def make(sizes):
    n_x, n_core, n_z, n_y = sizes
    n_col = n_z * n_y

    def swap(value):
        return lax.ppermute(value, "core", [(i, n_core - 1 - i) for i in range(n_core)])

    def exchange(value):
        return lax.all_to_all(value, ("z", "y"), 0, 0)

    def parts_over_x(value):
        return [value] + [
            lax.ppermute(value, "x", [(i, (i + k) % n_x) for i in range(n_x)])
            for k in (1, n_x - 1, 2)
        ]

    def per_device(factor, pattern, rhs_trail, coupling, inverse, rhs):
        columns, height, width = rhs.shape
        share = width // (n_core * n_col)
        size = inverse.shape[1]
        block = n_col * size
        core = lax.axis_index("core")
        col = lax.axis_index("z") * n_y + lax.axis_index("y")

        tied = lax.optimization_barrier
        across = coupling.transpose(0, 1, 3, 2)
        packed = pack(EARLY, n_col, inverse, across)
        early = exchange(packed)
        packed_late = pack(LATE, n_col, inverse, across, after=[packed])
        right = lax.dynamic_slice(
            rhs, (0, 0, col * n_core * share), (columns, height, n_core * share)
        ).transpose(0, 2, 1)
        rights = [
            lax.dynamic_slice(right, (0, which * share, 0), (columns, share, height))
            for which in (core, 1 - core)
        ]
        rights = jnp.stack([rights[0], swap(rights[1])], axis=1)

        partial_shape = jax.ShapeDtypeStruct((share, block), jnp.float32)
        half_shape = jax.ShapeDtypeStruct((share, block // n_core), jnp.bfloat16)
        mark_shape = jax.ShapeDtypeStruct((8, 128), jnp.float32)
        early_both = (early, swap(early))
        keep, give, mark = call(
            lambda *refs: first_kernel(size, *refs),
            (partial_shape, partial_shape, mark_shape),
            right[0],
            early,
            scratch=[pltpu.VMEM((n_core * share, block), jnp.float32)],
            after=[rights, packed_late],
            name="first",
        )
        packed_late, mark = tied((packed_late, mark))
        late = exchange(packed_late)
        partial_sum = keep + swap(give)

        def send(halves_of, after):
            shape = (n_col, len(halves_of) // 2, n_core, share, block // n_core)
            bundle, mark = call(
                bundle_kernel,
                (jax.ShapeDtypeStruct(shape, jnp.bfloat16), mark_shape),
                    *halves_of,
                after=after,
                name="bundle",
            )
            return exchange(bundle), mark

        state, solved, sent = rights, [], []
        for column in range(1, columns + 1):
            parts = parts_over_x(partial_sum)
            *solved, keep, give, mark = call(
                lambda *refs: close_kernel(n_x, *refs),
                (
                    jax.ShapeDtypeStruct((column, share, block), jnp.bfloat16),
                    half_shape,
                    half_shape,
                    mark_shape,
                ),
                *parts,
                *solved,
                after=[mark],
                name="close",
            )
            sent += [keep, swap(give)]
            if column == columns:
                break
            if column == 1:
                group, starts = early_both, (size, size)
            elif column == 2:
                first_pair, sent_mark = send(sent, [])
                group = (late, swap(part(late, 0, 3 * size, [mark, sent_mark])))
                starts = (0, 0)
            else:
                group, starts = (late, other), (3 * size, 0)
            outs = [partial_shape]
            if column == 1:
                outs += [jax.ShapeDtypeStruct((columns + 1, *state.shape[1:]), state.dtype)]
            partial_sum, *more = call(
                lambda *refs, c=column, a=starts: step_kernel(c, a, size, *refs),
                outs,
                state,
                *solved,
                *group,
                name="step",
            )
            if column == 1:
                (state,) = more
            if column == 2:
                other = swap(part(late, 3 * size, 4 * size, [partial_sum]))

        second_pair, mark = send(sent[4:], [])
        first_pair, mark = tied((first_pair, mark))
        base, blocks = trail(
            (0, 1),
            pattern,
            rhs_trail,
            factor,
            first_pair,
            swap(first_pair),
            size,
            512,
            after=[mark],
        )
        second_pair, blocks = tied((second_pair, blocks))
        updated, blocks = trail(
            (2, 3),
            pattern,
            base,
            factor,
            second_pair,
            swap(second_pair),
            size,
            512,
            (blocks,),
        )
        return blocks, updated

    return per_device


def solution(mesh):
    row, col = mesh.shape["row"], mesh.shape["col"]
    sizes = (row // 2, 2, 4, col // 4)
    fine = Mesh(mesh.devices.reshape(sizes), ("x", "core", "z", "y"))
    r, c = ("x", "core"), ("z", "y")
    return jax.shard_map(
        make(sizes),
        mesh=fine,
        in_specs=(
            P(r + c, None, None, None),
            P(r + c, None),
            P(r + c, None, None),
            P(None, None, r, c),
            P(None, c, r),
            P(None, r, None),
        ),
        out_specs=(P(None, c, None), P(r + c, None, None)),
        check_vma=False,
    )
```

```python
import jax
import jax.numpy as jnp
from jax import lax
from jax.experimental import pallas as pl
from jax.experimental.pallas import tpu as pltpu
from jax.sharding import Mesh
from jax.sharding import PartitionSpec as P

NT = (((1,), (1,)), ((), ()))
NN = (((1,), (0,)), ((), ()))
MIB = 1024 * 1024
EARLY = ((0, None), (1, None), (1, 0))
LATE = ((2, None), (2, 0), (2, 1), (3, None), (3, 0), (3, 1), (3, 2))
REST = 16
LIMITS = (58, 54)


def core_of():
    return lax.axis_index("core")


def slab_of(core):
    return lax.axis_index("x") * lax.axis_size("core") + core


def col_of():
    return lax.axis_index("z") * lax.axis_size("y") + lax.axis_index("y")


def dot(a, b, dims):
    return lax.dot_general(a, b, dims, preferred_element_type=jnp.float32)


def call(kernel, outs, *operands, name, scratch=(), after=(), limit=24):
    vmem = pl.BlockSpec(memory_space=pltpu.VMEM)
    unread = pl.BlockSpec(memory_space=pl.ANY)
    count = len(operands)
    return pl.pallas_call(
        lambda *refs: kernel(*refs[:count], *refs[count + len(after) :]),
        out_shape=outs,
        in_specs=[vmem] * count + [unread] * len(after),
        out_specs=jax.tree.map(lambda _: vmem, outs),
        scratch_shapes=list(scratch),
        compiler_params=pltpu.CompilerParams(vmem_limit_bytes=limit * MIB),
        cost_estimate=pl.CostEstimate(
            flops=2**20, bytes_accessed=2**16, transcendentals=0
        ),
        name=name,
    )(*operands, *after)


def pack_kernel(members, inverse_ref, across_ref, out_ref):
    columns, rows, width = inverse_ref.shape
    blocks = []
    for column, earlier in members:
        if earlier is None:
            blocks.append(inverse_ref[column].astype(jnp.bfloat16))
        else:
            blocks.append(across_ref[column, earlier])
    if members[0][0] == 0:
        first_row, first_lane = col_of() * rows, slab_of(core_of()) * width
        on_diagonal = (
            lax.broadcasted_iota(jnp.int32, (rows, width), 0) + first_row
            == lax.broadcasted_iota(jnp.int32, (rows, width), 1) + first_lane
        )
        at_row = lax.broadcasted_iota(jnp.int32, (REST, width), 0)
        tile = jnp.zeros((REST, width), jnp.float32)
        for column in range(columns):
            value = inverse_ref[column]
            rest = value - value.astype(jnp.bfloat16).astype(jnp.float32)
            line = jnp.sum(jnp.where(on_diagonal, rest, 0.0), axis=0, keepdims=True)
            tile = tile + jnp.where(at_row == column, line, 0.0)
        blocks.append(tile.astype(jnp.bfloat16))
    whole = jnp.concatenate(blocks, axis=0)
    for copy in range(out_ref.shape[0]):
        out_ref[copy] = whole


def pack(members, copies, inverse, across, after=()):
    count = len(members) * inverse.shape[1] + (REST if members[0][0] == 0 else 0)
    shape = (copies, count, inverse.shape[2])

    def whole(shape):
        return pl.BlockSpec(shape, lambda i: (0,) * len(shape))

    held = 2
    return pl.pallas_call(
        lambda *refs: pack_kernel(members, *refs[:held], refs[-1]),
        grid=(1,),
        in_specs=[whole(inverse.shape), whole(across.shape)]
        + [pl.BlockSpec(memory_space=pl.ANY)] * len(after),
        out_specs=pl.BlockSpec(memory_space=pltpu.VMEM),
        out_shape=jax.ShapeDtypeStruct(shape, jnp.bfloat16),
        compiler_params=pltpu.CompilerParams(vmem_limit_bytes=24 * MIB),
        name="pack",
    )(inverse, across, *after)


def block_of(ref, at, size):
    return ref[:, at : at + size].reshape(ref.shape[0] * size, ref.shape[2])


def rest_of(ref, column):
    tiles = ref[:, ref.shape[1] - REST :].astype(jnp.float32)
    return jnp.sum(tiles, axis=0)[column : column + 1]


def apply_inverse(right, inverse, rest, slab, out_ref, add):
    count, width = right.shape
    high = right.astype(jnp.bfloat16)
    low = (right - high.astype(jnp.float32)).astype(jnp.bfloat16)
    both = dot(jnp.concatenate([high, low], axis=0), inverse, NT)
    value = both[:count] + both[count:]
    out_ref[...] = out_ref[...] + value if add else value
    lanes = pl.ds(pl.multiple_of(slab * width, width), width)
    out_ref[:, lanes] = out_ref[:, lanes] + right * rest


def first_kernel(
    size, right_ref, group_ref, keep_ref, give_ref, mark_ref, out_ref
):
    apply_inverse(
        right_ref[...],
        block_of(group_ref, 0, size),
        rest_of(group_ref, 0),
        slab_of(core_of()),
        out_ref,
        False,
    )
    count = keep_ref.shape[0]
    keep_ref[...] = out_ref[:count]
    give_ref[...] = out_ref[count:]
    mark_ref[...] = right_ref[: mark_ref.shape[0]]


def split_step_kernel(
    column, size, state_ref, solved_ref, got_ref, right_ref, group_ref, keep_ref, give_ref, out_ref
):
    right = right_ref[...]
    for i in range(column):
        both = jnp.concatenate([solved_ref[i], got_ref[i]], axis=0)
        right = right - dot(both, block_of(group_ref, (1 + i) * size, size), NN)
    apply_inverse(
        right,
        block_of(group_ref, 0, size),
        state_ref[state_ref.shape[0] - 1, 0, column : column + 1],
        slab_of(core_of()),
        out_ref,
        False,
    )
    count = keep_ref.shape[0]
    keep_ref[...] = out_ref[:count]
    give_ref[...] = out_ref[count:]


def part_kernel(start, group_ref, out_ref):
    out_ref[...] = group_ref[:, start : start + out_ref.shape[1]]


def part(group, start, length, after):
    shape = (group.shape[0], length, group.shape[2])
    return call(
        lambda *refs: part_kernel(start, *refs),
        jax.ShapeDtypeStruct(shape, group.dtype),
        group,
        after=after,
        name="part",
    )


def close_kernel(n_parts, n_before, *refs):
    part_refs, before_refs = refs[:n_parts], refs[n_parts : n_parts + n_before]
    solved_ref, mark_ref, *bundle_refs = refs[n_parts + n_before :]
    total = part_refs[0][...]
    for part_ref in part_refs[1:]:
        total = total + part_ref[...]
    last = solved_ref.shape[0] - 1
    for ref in before_refs:
        solved_ref[:last] = ref[...]
    solved_ref[last] = total.astype(jnp.bfloat16)
    mark_ref[...] = total[: mark_ref.shape[0], : mark_ref.shape[1]]
    for ref in bundle_refs:
        both = solved_ref[last - 1 :]
        for copy in range(ref.shape[0]):
            ref[copy] = both


def step_kernel(column, starts, size, state_ref, solved_ref, *refs):
    group_refs, out_ref = refs[:2], refs[2]
    columns = state_ref.shape[0]
    if column == 1:
        next_ref = refs[3]
        next_ref[:columns] = state_ref[...]
        for side, ref in enumerate(group_refs):
            tiles = ref[:, ref.shape[1] - REST :].astype(jnp.float32)
            next_ref[columns, side] = jnp.sum(tiles, axis=0)
        state_ref, columns = next_ref, columns + 1
    slabs = (slab_of(core_of()), slab_of(1 - core_of()))
    for side, (ref, start) in enumerate(zip(group_refs, starts)):
        right = state_ref[column, side]
        for i in range(column):
            right = right - dot(
                solved_ref[i], block_of(ref, start + (1 + i) * size, size), NN
            )
        apply_inverse(
            right,
            block_of(ref, start, size),
            state_ref[columns - 1, side, column : column + 1],
            slabs[side],
            out_ref,
            side > 0,
        )


def trail_kernel(columns, before, pattern_ref, base_ref, mine_ref, other_ref, *refs):
    count = len(columns)
    factor_refs, (out_ref, own_ref) = refs[:count], refs[-2:]
    row = pl.program_id(0)
    half, depth = out_ref.shape[2] // 2, mine_ref.shape[3]
    sides = []
    for ref, core in ((mine_ref, core_of()), (other_ref, 1 - core_of())):
        sides.append((ref, pl.ds(pl.multiple_of(core * half, half), half)))

    def solved(ref, k):
        return ref[:, k].reshape(half, depth)

    for ref, lanes in sides:
        total = base_ref[0, :, lanes].astype(jnp.float32)
        for k, column in enumerate(columns):
            product = dot(factor_refs[k][0, 0], solved(ref, k), NT)
            total = total - pattern_ref[row, column].astype(jnp.float32) * product
        out_ref[0, :, lanes] = total

    @pl.when((row == 0) & (pl.program_id(1) == 0))
    def _():
        own = own_ref.shape[1]
        lane = lax.broadcasted_iota(jnp.int32, (own, depth), 1)
        wanted = lax.broadcasted_iota(jnp.int32, (own, depth), 0) + col_of() * own
        pick = (lane == wanted).astype(jnp.bfloat16)
        if before:
            own_ref[:before] = refs[count][...]
        for k in range(count):
            for ref, lanes in sides:
                own_ref[before + k, :, lanes] = dot(pick, solved(ref, k), NT).astype(
                    jnp.bfloat16
                )


def trail(columns, pattern, base, factor, mine, other, own, tile, limit, done=(), after=()):
    n_rows, height, width = base.shape
    depth = factor.shape[-1]
    count, before = len(columns), sum(d.shape[0] for d in done)
    smem = pl.BlockSpec(memory_space=pltpu.SMEM)
    row_tile = pl.BlockSpec((1, tile, width), lambda r, a: (r, a, 0))

    def factor_spec(column):
        return pl.BlockSpec((1, 1, tile, depth), lambda r, a: (r, column, a, 0))

    def whole(shape):
        return pl.BlockSpec(shape, lambda r, a: (0,) * len(shape))

    held = 4 + count + len(done)
    own_shape = (before + count, own, width)
    return pl.pallas_call(
        lambda *refs: trail_kernel(columns, before, *refs[:held], *refs[-2:]),
        grid=(n_rows, height // tile),
        in_specs=[smem, row_tile] + [pl.BlockSpec(memory_space=pltpu.VMEM)] * 2
        + [factor_spec(column) for column in columns]
        + [whole(d.shape) for d in done]
        + [pl.BlockSpec(memory_space=pl.ANY)] * len(after),
        out_specs=[row_tile, whole(own_shape)],
        out_shape=[
            jax.ShapeDtypeStruct(base.shape, jnp.float32),
            jax.ShapeDtypeStruct(own_shape, jnp.bfloat16),
        ],
        compiler_params=pltpu.CompilerParams(vmem_limit_bytes=limit * MIB),
        cost_estimate=pl.CostEstimate(
            flops=2 * n_rows * height * width * depth * count,
            bytes_accessed=2 * n_rows * height * depth * count,
            transcendentals=0,
        ),
        name="trail",
    )(pattern, base, mine, other, *([factor] * count), *done, *after)


def make(sizes):
    n_x, n_core, n_z, n_y = sizes
    n_col = n_z * n_y

    def swap(value):
        return lax.ppermute(value, "core", [(i, n_core - 1 - i) for i in range(n_core)])

    def exchange(value):
        return lax.all_to_all(value, ("z", "y"), 0, 0)

    def parts_over_x(value):
        return [value] + [
            lax.ppermute(value, "x", [(i, (i + k) % n_x) for i in range(n_x)])
            for k in (1, n_x - 1, 2)
        ]

    def per_device(factor, pattern, rhs_trail, coupling, inverse, rhs):
        columns, height, width = rhs.shape
        share = width // (n_core * n_col)
        size = inverse.shape[1]
        block = n_col * size
        core = lax.axis_index("core")
        col = lax.axis_index("z") * n_y + lax.axis_index("y")

        tied = lax.optimization_barrier
        across = coupling.transpose(0, 1, 3, 2)
        packed = pack(EARLY, n_col, inverse, across)
        early = exchange(packed)
        packed_late = pack(LATE, n_col, inverse, across, after=[packed])
        def columns_of(which):
            at = (which * n_col + col) * share
            return lax.dynamic_slice(
                rhs, (0, 0, at), (columns, height, share)
            ).transpose(0, 2, 1)

        mine, theirs = columns_of(core), columns_of(1 - core)
        rights = jnp.stack([mine, swap(theirs)], axis=1)
        right = jnp.concatenate([mine[0], theirs[0]])

        partial_shape = jax.ShapeDtypeStruct((share, block), jnp.float32)
        mark_shape = jax.ShapeDtypeStruct((8, 128), jnp.float32)
        keep, give, mark = call(
            lambda *refs: first_kernel(size, *refs),
            (partial_shape, partial_shape, mark_shape),
            right,
            early,
            scratch=[pltpu.VMEM((n_core * share, block), jnp.float32)],
            after=[rights, packed_late],
            name="first",
        )
        packed_late, mark = tied((packed_late, mark))
        late = exchange(packed_late)
        partial_sum = keep + swap(give)
        early_part = part(early, size, 2 * size + REST, [partial_sum])

        state, solved = rights, []
        bundle_shape = jax.ShapeDtypeStruct((n_col, 2, share, block), jnp.bfloat16)
        for column in range(1, columns + 1):
            parts = parts_over_x(partial_sum)
            now, mark, *bundle = call(
                lambda *refs, n=len(solved): close_kernel(n_x, n, *refs),
                [jax.ShapeDtypeStruct((column, share, block), jnp.bfloat16), mark_shape]
                + [bundle_shape] * (column % 2 == 0),
                *parts,
                *solved,
                after=[mark],
                name="close",
            )
            solved = [now]
            if column == 4:
                first_pair, mark = tied((first_pair, mark))
            if column == columns:
                break
            if column == 1:
                group, starts = (early, swap(early_part)), (size, 0)
            elif column == 2:
                first_pair = exchange(bundle[0])
                keep, give = call(
                    lambda *refs: split_step_kernel(2, size, *refs),
                    (partial_shape, partial_shape),
                    state,
                    now,
                    swap(now),
                    jnp.concatenate([mine[2], theirs[2]]),
                    late,
                    scratch=[pltpu.VMEM((n_core * share, block), jnp.float32)],
                    name="split",
                )
                partial_sum = keep + swap(give)
                other = swap(part(late, 3 * size, 4 * size, [partial_sum]))
                continue
            else:
                group, starts = (late, other), (3 * size, 0)
            outs = [partial_shape]
            if column == 1:
                outs += [jax.ShapeDtypeStruct((columns + 1, *state.shape[1:]), state.dtype)]
            partial_sum, *more = call(
                lambda *refs, c=column, a=starts: step_kernel(c, a, size, *refs),
                outs,
                state,
                *solved,
                *group,
                name="step",
            )
            if column == 1:
                (state,) = more

        second_pair = exchange(bundle[0])
        base, blocks = trail(
            (0, 1),
            pattern,
            rhs_trail,
            factor,
            first_pair,
            swap(first_pair),
            size,
            512,
            LIMITS[0],
            after=[mark],
        )
        second_pair, blocks = tied((second_pair, blocks))
        updated, blocks = trail(
            (2, 3),
            pattern,
            base,
            factor,
            second_pair,
            swap(second_pair),
            size,
            512,
            LIMITS[1],
            (blocks,),
        )
        return blocks, updated

    return per_device


def solution(mesh):
    row, col = mesh.shape["row"], mesh.shape["col"]
    sizes = (row // 2, 2, 4, col // 4)
    fine = Mesh(mesh.devices.reshape(sizes), ("x", "core", "z", "y"))
    r, c = ("x", "core"), ("z", "y")
    return jax.shard_map(
        make(sizes),
        mesh=fine,
        in_specs=(
            P(r + c, None, None, None),
            P(r + c, None),
            P(r + c, None, None),
            P(None, None, r, c),
            P(None, c, r),
            P(None, r, None),
        ),
        out_specs=(P(None, c, None), P(r + c, None, None)),
        check_vma=False,
    )
```

```python
import jax
import jax.numpy as jnp
from jax import lax
from jax.experimental import pallas as pl
from jax.experimental.pallas import tpu as pltpu
from jax.sharding import Mesh
from jax.sharding import PartitionSpec as P

NT = (((1,), (1,)), ((), ()))
NN = (((1,), (0,)), ((), ()))
MIB = 1024 * 1024
EARLY = ((0, None), (1, None), (1, 0))
LATE = ((2, None), (2, 0), (2, 1), (3, None), (3, 0), (3, 1), (3, 2))
REST = 16
LIMITS = (58, 54)


def core_of():
    return lax.axis_index("core")


def slab_of(core):
    return lax.axis_index("x") * lax.axis_size("core") + core


def col_of():
    return lax.axis_index("z") * lax.axis_size("y") + lax.axis_index("y")


def dot(a, b, dims):
    return lax.dot_general(a, b, dims, preferred_element_type=jnp.float32)


def call(kernel, outs, *operands, name, scratch=(), after=(), limit=24):
    vmem = pl.BlockSpec(memory_space=pltpu.VMEM)
    unread = pl.BlockSpec(memory_space=pl.ANY)
    count = len(operands)
    return pl.pallas_call(
        lambda *refs: kernel(*refs[:count], *refs[count + len(after) :]),
        out_shape=outs,
        in_specs=[vmem] * count + [unread] * len(after),
        out_specs=jax.tree.map(lambda _: vmem, outs),
        scratch_shapes=list(scratch),
        compiler_params=pltpu.CompilerParams(vmem_limit_bytes=limit * MIB),
        cost_estimate=pl.CostEstimate(
            flops=2**20, bytes_accessed=2**16, transcendentals=0
        ),
        name=name,
    )(*operands, *after)


def pack_kernel(members, inverse_ref, across_ref, out_ref):
    columns, rows, width = inverse_ref.shape
    blocks = []
    for column, earlier in members:
        if earlier is None:
            blocks.append(inverse_ref[column].astype(jnp.bfloat16))
        else:
            blocks.append(across_ref[column, earlier])
    if members[0][0] == 0:
        first_row, first_lane = col_of() * rows, slab_of(core_of()) * width
        on_diagonal = (
            lax.broadcasted_iota(jnp.int32, (rows, width), 0) + first_row
            == lax.broadcasted_iota(jnp.int32, (rows, width), 1) + first_lane
        )
        at_row = lax.broadcasted_iota(jnp.int32, (REST, width), 0)
        tile = jnp.zeros((REST, width), jnp.float32)
        for column in range(columns):
            value = inverse_ref[column]
            rest = value - value.astype(jnp.bfloat16).astype(jnp.float32)
            line = jnp.sum(jnp.where(on_diagonal, rest, 0.0), axis=0, keepdims=True)
            tile = tile + jnp.where(at_row == column, line, 0.0)
        blocks.append(tile.astype(jnp.bfloat16))
    whole = jnp.concatenate(blocks, axis=0)
    for copy in range(out_ref.shape[0]):
        out_ref[copy] = whole


def pack(members, copies, inverse, across, after=()):
    count = len(members) * inverse.shape[1] + (REST if members[0][0] == 0 else 0)
    shape = (copies, count, inverse.shape[2])

    def kernel(inverse_from, across_from, *refs):
        out_ref, inverse_ref, across_ref, sems = refs[-4:]
        moves = [
            pltpu.make_async_copy(inverse_from, inverse_ref, sems.at[0]),
            pltpu.make_async_copy(across_from, across_ref, sems.at[1]),
        ]
        for move in moves:
            move.start()
        for move in moves:
            move.wait()
        pack_kernel(members, inverse_ref, across_ref, out_ref)

    return pl.pallas_call(
        kernel,
        in_specs=[pl.BlockSpec(memory_space=pltpu.HBM)] * 2
        + [pl.BlockSpec(memory_space=pl.ANY)] * len(after),
        out_specs=pl.BlockSpec(memory_space=pltpu.VMEM),
        out_shape=jax.ShapeDtypeStruct(shape, jnp.bfloat16),
        scratch_shapes=[
            pltpu.VMEM(inverse.shape, inverse.dtype),
            pltpu.VMEM(across.shape, across.dtype),
            pltpu.SemaphoreType.DMA((2,)),
        ],
        compiler_params=pltpu.CompilerParams(vmem_limit_bytes=(24 if after else 63) * MIB),
        name="pack",
    )(inverse, across, *after)


def block_of(ref, at, size):
    return ref[:, at : at + size].reshape(ref.shape[0] * size, ref.shape[2])


def rest_of(ref, column):
    tiles = ref[:, ref.shape[1] - REST :].astype(jnp.float32)
    return jnp.sum(tiles, axis=0)[column : column + 1]


def apply_inverse(right, inverse, rest, slab, out_ref, add):
    count, width = right.shape
    high = right.astype(jnp.bfloat16)
    low = (right - high.astype(jnp.float32)).astype(jnp.bfloat16)
    both = dot(jnp.concatenate([high, low], axis=0), inverse, NT)
    value = both[:count] + both[count:]
    out_ref[...] = out_ref[...] + value if add else value
    lanes = pl.ds(pl.multiple_of(slab * width, width), width)
    out_ref[:, lanes] = out_ref[:, lanes] + right * rest


def first_kernel(
    size, right_ref, group_ref, keep_ref, give_ref, mark_ref, out_ref
):
    apply_inverse(
        right_ref[...],
        block_of(group_ref, 0, size),
        rest_of(group_ref, 0),
        slab_of(core_of()),
        out_ref,
        False,
    )
    count = keep_ref.shape[0]
    keep_ref[...] = out_ref[:count]
    give_ref[...] = out_ref[count:]
    mark_ref[...] = right_ref[: mark_ref.shape[0]]


def split_step_kernel(
    column, size, state_ref, solved_ref, got_ref, right_ref, group_ref, keep_ref, give_ref, out_ref
):
    right = right_ref[...]
    for i in range(column):
        both = jnp.concatenate([solved_ref[i], got_ref[i]], axis=0)
        right = right - dot(both, block_of(group_ref, (1 + i) * size, size), NN)
    apply_inverse(
        right,
        block_of(group_ref, 0, size),
        state_ref[state_ref.shape[0] - 1, 0, column : column + 1],
        slab_of(core_of()),
        out_ref,
        False,
    )
    count = keep_ref.shape[0]
    keep_ref[...] = out_ref[:count]
    give_ref[...] = out_ref[count:]


def part_kernel(start, group_ref, out_ref):
    out_ref[...] = group_ref[:, start : start + out_ref.shape[1]]


def part(group, start, length, after):
    shape = (group.shape[0], length, group.shape[2])
    return call(
        lambda *refs: part_kernel(start, *refs),
        jax.ShapeDtypeStruct(shape, group.dtype),
        group,
        after=after,
        name="part",
    )


def close_kernel(n_parts, n_before, *refs):
    part_refs, before_refs = refs[:n_parts], refs[n_parts : n_parts + n_before]
    solved_ref, mark_ref, *bundle_refs = refs[n_parts + n_before :]
    total = part_refs[0][...]
    for part_ref in part_refs[1:]:
        total = total + part_ref[...]
    last = solved_ref.shape[0] - 1
    for ref in before_refs:
        solved_ref[:last] = ref[...]
    solved_ref[last] = total.astype(jnp.bfloat16)
    mark_ref[...] = total[: mark_ref.shape[0], : mark_ref.shape[1]]
    for ref in bundle_refs:
        both = solved_ref[last - 1 :]
        for copy in range(ref.shape[0]):
            ref[copy] = both


def step_kernel(column, starts, size, state_ref, solved_ref, *refs):
    group_refs, out_ref = refs[:2], refs[2]
    columns = state_ref.shape[0]
    if column == 1:
        next_ref = refs[3]
        next_ref[:columns] = state_ref[...]
        for side, ref in enumerate(group_refs):
            tiles = ref[:, ref.shape[1] - REST :].astype(jnp.float32)
            next_ref[columns, side] = jnp.sum(tiles, axis=0)
        state_ref, columns = next_ref, columns + 1
    slabs = (slab_of(core_of()), slab_of(1 - core_of()))
    for side, (ref, start) in enumerate(zip(group_refs, starts)):
        right = state_ref[column, side]
        for i in range(column):
            right = right - dot(
                solved_ref[i], block_of(ref, start + (1 + i) * size, size), NN
            )
        apply_inverse(
            right,
            block_of(ref, start, size),
            state_ref[columns - 1, side, column : column + 1],
            slabs[side],
            out_ref,
            side > 0,
        )


def trail_kernel(columns, before, pattern_ref, base_ref, mine_ref, other_ref, *refs):
    count = len(columns)
    factor_refs, (out_ref, own_ref) = refs[:count], refs[-2:]
    row = pl.program_id(0)
    half, depth = out_ref.shape[2] // 2, mine_ref.shape[3]
    sides = []
    for ref, core in ((mine_ref, core_of()), (other_ref, 1 - core_of())):
        sides.append((ref, pl.ds(pl.multiple_of(core * half, half), half)))

    def solved(ref, k):
        return ref[:, k].reshape(half, depth)

    for ref, lanes in sides:
        total = base_ref[0, :, lanes].astype(jnp.float32)
        for k, column in enumerate(columns):
            product = dot(factor_refs[k][0, 0], solved(ref, k), NT)
            total = total - pattern_ref[row, column].astype(jnp.float32) * product
        out_ref[0, :, lanes] = total

    @pl.when((row == 0) & (pl.program_id(1) == 1))
    def _():
        own = own_ref.shape[1]
        lane = lax.broadcasted_iota(jnp.int32, (own, depth), 1)
        wanted = lax.broadcasted_iota(jnp.int32, (own, depth), 0) + col_of() * own
        pick = (lane == wanted).astype(jnp.bfloat16)
        if before:
            own_ref[:before] = refs[count][...]
        for k in range(count):
            for ref, lanes in sides:
                own_ref[before + k, :, lanes] = dot(pick, solved(ref, k), NT).astype(
                    jnp.bfloat16
                )


def trail(columns, pattern, base, factor, mine, other, own, tile, limit, done=(), after=()):
    n_rows, height, width = base.shape
    depth = factor.shape[-1]
    count, before = len(columns), sum(d.shape[0] for d in done)
    smem = pl.BlockSpec(memory_space=pltpu.SMEM)
    row_tile = pl.BlockSpec((1, tile, width), lambda r, a: (r, a, 0))

    def factor_spec(column):
        return pl.BlockSpec((1, 1, tile, depth), lambda r, a: (r, column, a, 0))

    def whole(shape):
        return pl.BlockSpec(shape, lambda r, a: (0,) * len(shape))

    held = 4 + count + len(done)
    own_shape = (before + count, own, width)
    return pl.pallas_call(
        lambda *refs: trail_kernel(columns, before, *refs[:held], *refs[-2:]),
        grid=(n_rows, height // tile),
        in_specs=[smem, row_tile] + [pl.BlockSpec(memory_space=pltpu.VMEM)] * 2
        + [factor_spec(column) for column in columns]
        + [whole(d.shape) for d in done]
        + [pl.BlockSpec(memory_space=pl.ANY)] * len(after),
        out_specs=[row_tile, whole(own_shape)],
        out_shape=[
            jax.ShapeDtypeStruct(base.shape, jnp.float32),
            jax.ShapeDtypeStruct(own_shape, jnp.bfloat16),
        ],
        compiler_params=pltpu.CompilerParams(vmem_limit_bytes=limit * MIB),
        cost_estimate=pl.CostEstimate(
            flops=2 * n_rows * height * width * depth * count,
            bytes_accessed=2 * n_rows * height * depth * count,
            transcendentals=0,
        ),
        name="trail",
    )(pattern, base, mine, other, *([factor] * count), *done, *after)


def make(sizes):
    n_x, n_core, n_z, n_y = sizes
    n_col = n_z * n_y

    def swap(value):
        return lax.ppermute(value, "core", [(i, n_core - 1 - i) for i in range(n_core)])

    def exchange(value):
        return lax.all_to_all(value, ("z", "y"), 0, 0)

    def parts_over_x(value):
        return [value] + [
            lax.ppermute(value, "x", [(i, (i + k) % n_x) for i in range(n_x)])
            for k in (1, n_x - 1, 2)
        ]

    def per_device(factor, pattern, rhs_trail, coupling, inverse, rhs):
        columns, height, width = rhs.shape
        share = width // (n_core * n_col)
        size = inverse.shape[1]
        block = n_col * size
        core = lax.axis_index("core")
        col = lax.axis_index("z") * n_y + lax.axis_index("y")

        tied = lax.optimization_barrier
        across = coupling.transpose(0, 1, 3, 2)
        packed = pack(EARLY, n_col, inverse, across)
        early = exchange(packed)
        packed_late = pack(LATE, n_col, inverse, across, after=[packed])
        def columns_of(which):
            at = (which * n_col + col) * share
            return lax.dynamic_slice(
                rhs, (0, 0, at), (columns, height, share)
            ).transpose(0, 2, 1)

        mine, theirs = columns_of(core), columns_of(1 - core)
        rights = jnp.stack([mine, swap(theirs)], axis=1)
        right = jnp.concatenate([mine[0], theirs[0]])

        partial_shape = jax.ShapeDtypeStruct((share, block), jnp.float32)
        mark_shape = jax.ShapeDtypeStruct((8, 128), jnp.float32)
        keep, give, mark = call(
            lambda *refs: first_kernel(size, *refs),
            (partial_shape, partial_shape, mark_shape),
            right,
            early,
            scratch=[pltpu.VMEM((n_core * share, block), jnp.float32)],
            after=[rights, packed_late],
            name="first",
        )
        packed_late, mark = tied((packed_late, mark))
        late = exchange(packed_late)
        partial_sum = keep + swap(give)
        early_part = part(early, size, 2 * size + REST, [partial_sum])

        state, solved = rights, []
        bundle_shape = jax.ShapeDtypeStruct((n_col, 2, share, block), jnp.bfloat16)
        for column in range(1, columns + 1):
            parts = parts_over_x(partial_sum)
            now, mark, *bundle = call(
                lambda *refs, n=len(solved): close_kernel(n_x, n, *refs),
                [jax.ShapeDtypeStruct((column, share, block), jnp.bfloat16), mark_shape]
                + [bundle_shape] * (column % 2 == 0),
                *parts,
                *solved,
                after=[mark],
                name="close",
            )
            solved = [now]
            if column == 4:
                first_pair, mark = tied((first_pair, mark))
            if column == columns:
                break
            if column == 1:
                group, starts = (early, swap(early_part)), (size, 0)
            elif column == 2:
                first_pair = exchange(bundle[0])
                keep, give = call(
                    lambda *refs: split_step_kernel(2, size, *refs),
                    (partial_shape, partial_shape),
                    state,
                    now,
                    swap(now),
                    jnp.concatenate([mine[2], theirs[2]]),
                    late,
                    scratch=[pltpu.VMEM((n_core * share, block), jnp.float32)],
                    name="split",
                )
                partial_sum = keep + swap(give)
                other = swap(part(late, 3 * size, 4 * size, [partial_sum]))
                continue
            else:
                group, starts = (late, other), (3 * size, 0)
            outs = [partial_shape]
            if column == 1:
                outs += [jax.ShapeDtypeStruct((columns + 1, *state.shape[1:]), state.dtype)]
            partial_sum, *more = call(
                lambda *refs, c=column, a=starts: step_kernel(c, a, size, *refs),
                outs,
                state,
                *solved,
                *group,
                name="step",
            )
            if column == 1:
                (state,) = more

        second_pair = exchange(bundle[0])
        base, blocks = trail(
            (0, 1),
            pattern,
            rhs_trail,
            factor,
            first_pair,
            swap(first_pair),
            size,
            512,
            LIMITS[0],
            after=[mark],
        )
        second_pair, blocks = tied((second_pair, blocks))
        updated, blocks = trail(
            (2, 3),
            pattern,
            base,
            factor,
            second_pair,
            swap(second_pair),
            size,
            512,
            LIMITS[1],
            (blocks,),
        )
        return blocks, updated

    return per_device


def solution(mesh):
    row, col = mesh.shape["row"], mesh.shape["col"]
    sizes = (row // 2, 2, 4, col // 4)
    fine = Mesh(mesh.devices.reshape(sizes), ("x", "core", "z", "y"))
    r, c = ("x", "core"), ("z", "y")
    return jax.shard_map(
        make(sizes),
        mesh=fine,
        in_specs=(
            P(r + c, None, None, None),
            P(r + c, None),
            P(r + c, None, None),
            P(None, None, r, c),
            P(None, c, r),
            P(None, r, None),
        ),
        out_specs=(P(None, c, None), P(r + c, None, None)),
        check_vma=False,
    )
```
